32 devices in a mesh: grp: 2 (over x), row: 8 (over z, y), col: 2 (over core).
Axes of the slice: x: 2, y: 2, z: 4, core: 2. Of those that a mesh axis runs over, the one named last changes fastest.
Arguments:
- x_codes: bfloat16 [4096, 16384], P(('grp', 'col'), 'row'), parts along dimension 0, may hold values from -6 to 6
- x_scale: bfloat16 [4096, 128], P(('grp', 'col'), 'row'), parts along dimension 0, may hold values from 0.5 to 2
- grad_codes: bfloat16 [4096, 16384], P(('grp', 'col'), 'row'), parts along dimension 0, may hold values from -6 to 6
- grad_scale: bfloat16 [4096, 128], P(('grp', 'col'), 'row'), parts along dimension 0, may hold values from 0.5 to 2
- gate_pre: bfloat16 [4096, 2048], P(('grp', 'row'), 'col'), parts along dimension 0, may hold values from -6 to 6
- up_pre: bfloat16 [4096, 2048], P(('grp', 'row'), 'col'), parts along dimension 0, may hold values from -6 to 6
- w_gate: bfloat16 [16384, 2048], P('row', 'col'), may hold values from -0.046875 to 0.046875
- gate_scale: float32 [128, 16], P('row', 'col'), may hold values from 0.5 to 2
- w_up: bfloat16 [16384, 2048], P('row', 'col'), may hold values from -0.046875 to 0.046875
- up_scale: float32 [128, 16], P('row', 'col'), may hold values from 0.5 to 2
- w_down: bfloat16 [2048, 16384], P('col', 'row'), may hold values from -0.125 to 0.125
- down_scale: float32 [16, 128], P('col', 'row'), may hold values from 0.5 to 2
Outputs:
- grad_input: bfloat16 [4096, 16384], P(('grp', 'col'), 'row'), parts along dimension 0
- grad_gate: bfloat16 [32768, 2048], P(('grp', 'row'), 'col'), parts along dimension 0
- grad_up: bfloat16 [32768, 2048], P(('grp', 'row'), 'col'), parts along dimension 0
- grad_down: bfloat16 [4096, 16384], P(('grp', 'col'), 'row'), parts along dimension 0
The draws below stay inside these ranges and needn't reach their ends.
There are 2 independent parts, one for each index of `grp`. The reference program is written for one: setup_inputs(seed, part) draws one part's arguments, and reference() takes and returns one part's arrays. A program takes and returns all parts, laid end to end along the dimension named above; an argument that names none is the same for every part. Nothing has to cross between parts.
All inputs are finite; a program needn't handle non-finite values.
Results may differ from the reference program's by a relative error of at most 0.007.
Values may be sent and summed in bfloat16 or wider, within the bound.
A program may use at most 256 MiB of HBM per device.

```python
import math
import jax
import jax.numpy as jnp
from jax import lax

D = 16384
F = 2048
TOKENS = 2048


def block_scale(rng, extent, pieces, least, high):
    def one(dim, shards_of):
        steps = jax.random.uniform(jax.random.fold_in(jax.random.fold_in(rng, 6), dim), (shards_of,), jnp.float32, least / len(pieces), high / len(pieces))
        return jnp.repeat(jnp.exp(steps), extent[dim] // shards_of).reshape((-1,) + (1,) * (len(extent) - dim - 1))

    loudness = one(*pieces[0])
    for cut in pieces[1:]:
        loudness = loudness * one(*cut)
    return loudness


def bell_draw(own_key, dims, scale, reach, shards=(), kind=jnp.bfloat16):
    array = scale * jax.random.normal(own_key, dims, jnp.float32)
    if shards:
        array = array * block_scale(own_key, dims, shards, -0.22, 0.18)
    return jnp.clip(array, -reach, reach).astype(kind)


def setup_inputs(seed: int = 0, part: int = 0) -> dict:
    seeds = jax.random.split(jax.random.key(seed), 13)
    part_splits = jax.random.split(jax.random.fold_in(seeds[12], part), 13)
    x_codes = bell_draw(part_splits[0], (TOKENS, D), 1.0, 6.0, ((0, 2), (1, 8)))
    x_scale = jnp.clip(jnp.exp(math.log(2.0) - 1.3862944 * jax.random.uniform(part_splits[1], (TOKENS, D // 128), jnp.float32) ** block_scale(part_splits[1], (TOKENS, D // 128), ((0, 2), (1, 8)), -0.2, 0.2)), 0.5, 2.0).astype(jnp.bfloat16)
    grad_codes = bell_draw(part_splits[2], (TOKENS, D), 1.0, 6.0, ((0, 2), (1, 8)))
    grad_scale = jnp.clip(jnp.exp(math.log(2.0) - 1.3862944 * jax.random.uniform(part_splits[3], (TOKENS, D // 128), jnp.float32) ** block_scale(part_splits[3], (TOKENS, D // 128), ((0, 2), (1, 8)), -0.2, 0.2)), 0.5, 2.0).astype(jnp.bfloat16)
    gate_pre = bell_draw(part_splits[4], (TOKENS, F), 1.5, 6.0, ((0, 8), (1, 2)))
    up_pre = bell_draw(part_splits[5], (TOKENS, F), 1.0, 6.0, ((0, 8), (1, 2)))
    w_gate = bell_draw(seeds[6], (D, F), D ** -0.5, 0.046875, ((0, 8), (1, 2)))
    gate_scale = jnp.clip(jnp.exp(math.log(2.0) - 1.3862944 * jax.random.uniform(seeds[7], (D // 128, F // 128), jnp.float32) ** block_scale(seeds[7], (D // 128, F // 128), ((0, 8), (1, 2)), -0.2, 0.2)), 0.5, 2.0)
    w_up = bell_draw(seeds[8], (D, F), D ** -0.5, 0.046875, ((0, 8), (1, 2)))
    up_scale = jnp.clip(jnp.exp(math.log(2.0) - 1.3862944 * jax.random.uniform(seeds[9], (D // 128, F // 128), jnp.float32) ** block_scale(seeds[9], (D // 128, F // 128), ((0, 8), (1, 2)), -0.2, 0.2)), 0.5, 2.0)
    w_down = bell_draw(seeds[10], (F, D), F ** -0.5, 0.125, ((0, 2), (1, 8)))
    down_scale = jnp.clip(jnp.exp(math.log(2.0) - 1.3862944 * jax.random.uniform(seeds[11], (F // 128, D // 128), jnp.float32) ** block_scale(seeds[11], (F // 128, D // 128), ((0, 2), (1, 8)), -0.2, 0.2)), 0.5, 2.0)
    return dict(x_codes=x_codes, x_scale=x_scale, grad_codes=grad_codes, grad_scale=grad_scale, gate_pre=gate_pre, up_pre=up_pre, w_gate=w_gate, gate_scale=gate_scale, w_up=w_up, up_scale=up_scale, w_down=w_down, down_scale=down_scale)


block_edge = 128

def rows_dequant(codes, scale):
    count, width = codes.shape
    parts = codes.astype(jnp.float32).reshape(count, width // block_edge, block_edge)
    return (parts * scale.astype(jnp.float32)[:, :, None]).reshape(count, width).astype(jnp.bfloat16)

def tile_dequant(codes, scale):
    height, width = codes.shape
    parts = codes.astype(jnp.float32).reshape(height // block_edge, block_edge, width // block_edge, block_edge)
    return (parts * scale.astype(jnp.float32)[:, None, :, None]).reshape(height, width).astype(jnp.bfloat16)

def swiglu_back(hidden_grad, gate_pre, up_pre):
    gate_val = gate_pre.astype(jnp.float32)
    up_val = up_pre.astype(jnp.float32)
    sigma = jax.nn.sigmoid(gate_val)
    active = gate_val * sigma
    hidden = (active * up_val).astype(jnp.bfloat16)
    up_grad = (hidden_grad * active).astype(jnp.bfloat16)
    gate_grad = (hidden_grad * up_val * sigma * (1.0 + gate_val * (1.0 - sigma))).astype(jnp.bfloat16)
    return (hidden, gate_grad, up_grad)

def reference(x_codes, x_scale, grad_codes, grad_scale, gate_pre, up_pre, w_gate, gate_scale, w_up, up_scale, w_down, down_scale):
    inputs = rows_dequant(x_codes, x_scale)
    out_grad = rows_dequant(grad_codes, grad_scale)
    gate_full = tile_dequant(w_gate, gate_scale)
    up_full = tile_dequant(w_up, up_scale)
    down_full = tile_dequant(w_down, down_scale)
    inner = (((1,), (1,)), ((), ()))
    outer = (((0,), (0,)), ((), ()))
    hidden_grad = lax.dot_general(out_grad, down_full, inner, preferred_element_type=jnp.float32)
    hidden, gate_grad, up_grad = swiglu_back(hidden_grad, gate_pre, up_pre)
    grad_input = lax.dot_general(gate_grad, gate_full, inner, preferred_element_type=jnp.float32)
    grad_input = grad_input + lax.dot_general(up_grad, up_full, inner, preferred_element_type=jnp.float32)
    factor = jnp.float32(1.0) / jnp.sqrt(jnp.float32(TOKENS))
    grad_gate = lax.dot_general(inputs, gate_grad, outer, preferred_element_type=jnp.float32) * factor
    grad_up = lax.dot_general(inputs, up_grad, outer, preferred_element_type=jnp.float32) * factor
    grad_down = lax.dot_general(hidden, out_grad, outer, preferred_element_type=jnp.float32) * factor
    return (grad_input.astype(jnp.bfloat16), grad_gate.astype(jnp.bfloat16), grad_up.astype(jnp.bfloat16), grad_down.astype(jnp.bfloat16))
```

```python
import jax
import jax.numpy as jnp
from jax import lax
from jax.sharding import PartitionSpec as P

block_edge = 128
f32, bf16 = jnp.float32, jnp.bfloat16
inner = (((1,), (1,)), ((), ()))
outer = (((0,), (0,)), ((), ()))


def rows_dequant(codes, scale):
    count, width = codes.shape
    parts = codes.astype(f32).reshape(count, width // block_edge, block_edge)
    return (parts * scale.astype(f32)[:, :, None]).reshape(count, width).astype(bf16)


def tile_dequant(codes, scale):
    height, width = codes.shape
    parts = codes.astype(f32).reshape(
        height // block_edge, block_edge, width // block_edge, block_edge
    )
    return (parts * scale[:, None, :, None]).reshape(height, width).astype(bf16)


def dot(a, b, dims):
    return lax.dot_general(a, b, dims, preferred_element_type=f32)


def local(rows, *args):
    (
        x_codes,
        x_scale,
        grad_codes,
        grad_scale,
        gate_pre,
        up_pre,
        w_gate,
        gate_scale,
        w_up,
        up_scale,
        w_down,
        down_scale,
    ) = args
    line = rows // 2
    row = lax.axis_index("row")
    col = lax.axis_index("col")
    y, z = row % 2, row // 2
    swap_col = [(0, 1), (1, 0)]
    swap_y = [(i, i ^ 1) for i in range(rows)]

    def shift_z(k):
        return [(i, (i + 2 * k) % rows) for i in range(rows)]

    gate_all = lax.all_gather(gate_pre, "row", axis=0, tiled=True)
    up_all = lax.all_gather(up_pre, "row", axis=0, tiled=True)

    grad_own = rows_dequant(grad_codes, grad_scale)
    grad_other = lax.ppermute(grad_own, "col", swap_col)
    down_full = tile_dequant(w_down, down_scale)
    half = grad_own.shape[0]
    tokens = 2 * half
    chunk = tokens // rows
    units = down_full.shape[0]

    pieces = 2
    wide = units // pieces
    mine = []
    for j in range(pieces):
        down = down_full[j * wide : (j + 1) * wide]
        own = dot(grad_own, down, inner).reshape(line // 2, 2, chunk, wide)
        other = dot(grad_other, down, inner).reshape(line // 2, 2, chunk, wide)
        sums = []
        for part in (own, other):
            away = lax.dynamic_index_in_dim(part, 1 - y, 1, keepdims=False).astype(bf16)
            keep = lax.dynamic_index_in_dim(part, y, 1, keepdims=False)
            sums.append(keep + lax.ppermute(away, "row", swap_y).astype(f32))
        low = jnp.where(col == 0, sums[0], sums[1])
        high = jnp.where(col == 0, sums[1], sums[0])
        both = jnp.concatenate([low, high], axis=0)
        packed = both.astype(bf16)
        total = lax.dynamic_index_in_dim(both, z, 0, keepdims=False)
        for k in range(1, line):
            send = lax.dynamic_index_in_dim(packed, (z + k) % line, 0, keepdims=False)
            total = total + lax.ppermute(send, "row", shift_z(k)).astype(f32)
        mine.append(total.astype(bf16))
    hidden_grad = lax.all_gather(
        jnp.concatenate(mine, axis=1), "row", axis=0, tiled=True
    ).astype(f32)

    inputs = lax.all_gather(rows_dequant(x_codes, x_scale), "col", axis=0, tiled=True)
    out_grad = lax.all_gather(grad_own, "col", axis=0, tiled=True)
    factor = f32(1.0) / jnp.sqrt(f32(tokens))

    gate_val, up_val = gate_all.astype(f32), up_all.astype(f32)
    sigma = jax.nn.sigmoid(gate_val)
    active = gate_val * sigma
    hidden = (active * up_val).astype(bf16)
    slope = (up_val * sigma * (1.0 + gate_val * (1.0 - sigma))).astype(bf16)
    hidden, active, slope = lax.optimization_barrier((hidden, active.astype(bf16), slope))
    grad_down = (dot(hidden, out_grad, outer) * factor).astype(bf16)

    gate_grad = (hidden_grad * slope.astype(f32)).astype(bf16)
    up_grad = (hidden_grad * active.astype(f32)).astype(bf16)
    gate_grad, up_grad = lax.optimization_barrier((gate_grad, up_grad))
    gate_full = tile_dequant(w_gate, gate_scale)
    up_full = tile_dequant(w_up, up_scale)

    def input_part(which):
        gate = lax.dynamic_slice_in_dim(gate_grad, which * half, half, 0)
        up = lax.dynamic_slice_in_dim(up_grad, which * half, half, 0)
        return dot(gate, gate_full, inner) + dot(up, up_full, inner)

    away = input_part(1 - col).astype(bf16)
    back = lax.ppermute(away, "col", swap_col)
    grad_gate = (dot(inputs, gate_grad, outer) * factor).astype(bf16)
    grad_up = (dot(inputs, up_grad, outer) * factor).astype(bf16)
    grad_input = (input_part(col) + back.astype(f32)).astype(bf16)
    return (grad_input, grad_gate, grad_up, grad_down)


def solution(mesh):
    rows = mesh.shape["row"]
    return jax.shard_map(
        lambda *args: local(rows, *args),
        mesh=mesh,
        in_specs=(
            P(("grp", "col"), "row"),
            P(("grp", "col"), "row"),
            P(("grp", "col"), "row"),
            P(("grp", "col"), "row"),
            P(("grp", "row"), "col"),
            P(("grp", "row"), "col"),
            P("row", "col"),
            P("row", "col"),
            P("row", "col"),
            P("row", "col"),
            P("col", "row"),
            P("col", "row"),
        ),
        out_specs=(
            P(("grp", "col"), "row"),
            P(("grp", "row"), "col"),
            P(("grp", "row"), "col"),
            P(("grp", "col"), "row"),
        ),
        check_vma=False,
    )
```

```python
import functools

import jax
import jax.numpy as jnp
from jax import lax
from jax.experimental import pallas as pl
from jax.experimental.pallas import tpu as pltpu
from jax.sharding import PartitionSpec as P

block_edge = 128
f32, bf16 = jnp.float32, jnp.bfloat16
inner = (((1,), (1,)), ((), ()))
outer = (((0,), (0,)), ((), ()))


def rows_dequant(codes, scale):
    count, width = codes.shape
    parts = codes.astype(f32).reshape(count, width // block_edge, block_edge)
    return (parts * scale.astype(f32)[:, :, None]).reshape(count, width).astype(bf16)


def tile_dequant(codes, scale):
    height, width = codes.shape
    parts = codes.astype(f32).reshape(
        height // block_edge, block_edge, width // block_edge, block_edge
    )
    return (parts * scale[:, None, :, None]).reshape(height, width).astype(bf16)


def dot(a, b, dims):
    return lax.dot_general(a, b, dims, preferred_element_type=f32)


def ring_kernel(
    rows,
    part,
    pre,
    out,
    pre_out,
    passed,
    arrived,
    sum_send,
    sum_recv,
    all_send,
    all_recv,
    pre_send,
    pre_recv,
):
    row = lax.axis_index("row")
    half = rows // 2
    wide = part.shape[2] // 2
    col = lax.axis_index("col")
    place = row // 2 + (row % 2) * (rows - 1 - 2 * (row // 2))

    def row_at(p):
        p = lax.rem(p + 2 * rows, rows)
        far = p // half
        return (1 - far) * (2 * p) + far * (2 * (rows - 1 - p) + 1)

    def own_part(r):
        return lax.rem(r + col * half, rows)

    ways = (1, -1)
    pre_out[row] = pre[...]
    barrier = pltpu.get_barrier_semaphore()
    for way in ways:
        pl.semaphore_signal(
            barrier,
            inc=1,
            device_id={"row": row_at(place + way)},
            device_id_type=pl.DeviceIdType.MESH,
        )
    pl.semaphore_wait(barrier, 2)

    def columns(d):
        return pl.ds(d * wide, wide)

    def push(d, src, dst, send, recv):
        copy = pltpu.make_async_remote_copy(
            src_ref=src,
            dst_ref=dst,
            send_sem=send,
            recv_sem=recv,
            device_id={"row": row_at(place + ways[d])},
            device_id_type=pl.DeviceIdType.MESH,
        )
        copy.start()
        return copy

    copies = []
    last = [None, None]
    before = [None, None]
    for s in range(rows - 1):
        for d in range(2):
            if s:
                last[d].wait_recv()
            term = part[own_part(row_at(place - ways[d] * (1 + s))), :, columns(d)]
            if s:
                term = term + arrived[d, s - 1].astype(f32)
            passed[d, s] = term.astype(bf16)
            last[d] = push(
                d, passed.at[d, s], arrived.at[d, s], sum_send.at[d, s], sum_recv.at[d, s]
            )
            copies.append(last[d])
        for d in range(2):
            if s:
                before[d].wait_recv()
            block = pre_out.at[row_at(place - ways[d] * s), :, columns(d)]
            before[d] = push(d, block, block, pre_send.at[d, s], pre_recv.at[d, s])
            copies.append(before[d])
    for s in range(rows - 1):
        for d in range(2):
            last[d].wait_recv()
            if s == 0:
                term = part[own_part(row), :, columns(d)] + arrived[d, rows - 2].astype(f32)
                out[row, :, columns(d)] = term.astype(bf16)
            block = out.at[row_at(place - ways[d] * s), :, columns(d)]
            last[d] = push(d, block, block, all_send.at[d, s], all_recv.at[d, s])
            copies.append(last[d])
    for d in range(2):
        before[d].wait_recv()
        last[d].wait_recv()
    for copy in copies:
        copy.wait_send()


def ring_total(rows, part, pre):
    chunk, units = part.shape[0] // rows, part.shape[1]
    steps = (2, rows - 1)
    out, pre_out = pl.pallas_call(
        functools.partial(ring_kernel, rows),
        out_shape=[jax.ShapeDtypeStruct((rows, chunk, units), bf16)] * 2,
        in_specs=[pl.BlockSpec(memory_space=pltpu.VMEM)] * 2,
        out_specs=[pl.BlockSpec(memory_space=pltpu.VMEM)] * 2,
        scratch_shapes=[
            pltpu.VMEM(steps + (chunk, units // 2), bf16),
            pltpu.VMEM(steps + (chunk, units // 2), bf16),
        ]
        + [pltpu.SemaphoreType.DMA(steps)] * 6,
        compiler_params=pltpu.CompilerParams(
            collective_id=0, has_side_effects=True, vmem_limit_bytes=40 * 2**20
        ),
        cost_estimate=pl.CostEstimate(
            flops=2 * part.size, bytes_accessed=300_000_000, transcendentals=0
        ),
    )(part.reshape(rows, chunk, units), pre)
    return out.reshape(rows * chunk, units), pre_out.reshape(rows * chunk, units)


def local(rows, *args):
    (
        x_codes,
        x_scale,
        grad_codes,
        grad_scale,
        gate_pre,
        up_pre,
        w_gate,
        gate_scale,
        w_up,
        up_scale,
        w_down,
        down_scale,
    ) = args
    col = lax.axis_index("col")
    swap_col = [(0, 1), (1, 0)]

    gate_all = lax.all_gather(gate_pre, "row", axis=0, tiled=True)

    grad_own = rows_dequant(grad_codes, grad_scale)
    grad_other = lax.ppermute(grad_own, "col", swap_col)
    down_full = tile_dequant(w_down, down_scale)
    half = grad_own.shape[0]
    tokens = 2 * half

    def in_order(own, other):
        whole = jnp.zeros((tokens, own.shape[1]), own.dtype)
        whole = lax.dynamic_update_slice_in_dim(whole, own, col * half, 0)
        return lax.dynamic_update_slice_in_dim(whole, other, (1 - col) * half, 0)

    hidden_part = jnp.zeros((tokens, down_full.shape[0]), f32)
    for place, grad in ((0, grad_own), (half, grad_other)):
        hidden_part = lax.dynamic_update_slice_in_dim(
            hidden_part, dot(grad, down_full, inner), place, 0
        )
    hidden_grad, up_all = ring_total(rows, hidden_part, up_pre)
    hidden_grad = hidden_grad.astype(f32)

    x_own = rows_dequant(x_codes, x_scale)
    inputs = in_order(x_own, lax.ppermute(x_own, "col", swap_col))
    out_grad = in_order(grad_own, grad_other)
    factor = f32(1.0) / jnp.sqrt(f32(tokens))

    gate_val, up_val = gate_all.astype(f32), up_all.astype(f32)
    sigma = jax.nn.sigmoid(gate_val)
    active = gate_val * sigma
    hidden = (active * up_val).astype(bf16)
    up_grad = (hidden_grad * active).astype(bf16)
    gate_grad = (hidden_grad * up_val * sigma * (1.0 + gate_val * (1.0 - sigma))).astype(bf16)
    grad_down = (dot(hidden, out_grad, outer) * factor).astype(bf16)
    gate_grad, up_grad = lax.optimization_barrier((gate_grad, up_grad))
    gate_full = tile_dequant(w_gate, gate_scale)
    up_full = tile_dequant(w_up, up_scale)

    def input_part(which):
        gate = lax.dynamic_slice_in_dim(gate_grad, which * half, half, 0)
        up = lax.dynamic_slice_in_dim(up_grad, which * half, half, 0)
        return dot(gate, gate_full, inner) + dot(up, up_full, inner)

    away = input_part(1 - col).astype(bf16)
    back = lax.ppermute(away, "col", swap_col)
    grad_gate = (dot(inputs, gate_grad, outer) * factor).astype(bf16)
    grad_up = (dot(inputs, up_grad, outer) * factor).astype(bf16)
    grad_input = (input_part(col) + back.astype(f32)).astype(bf16)
    return (grad_input, grad_gate, grad_up, grad_down)


def solution(mesh):
    rows = mesh.shape["row"]
    return jax.shard_map(
        lambda *args: local(rows, *args),
        mesh=mesh,
        in_specs=(
            P(("grp", "col"), "row"),
            P(("grp", "col"), "row"),
            P(("grp", "col"), "row"),
            P(("grp", "col"), "row"),
            P(("grp", "row"), "col"),
            P(("grp", "row"), "col"),
            P("row", "col"),
            P("row", "col"),
            P("row", "col"),
            P("row", "col"),
            P("col", "row"),
            P("col", "row"),
        ),
        out_specs=(
            P(("grp", "col"), "row"),
            P(("grp", "row"), "col"),
            P(("grp", "row"), "col"),
            P(("grp", "col"), "row"),
        ),
        check_vma=False,
    )
```
